128 devices in a mesh: pair: 8 (over y, core), chol: 16 (over z, x).
Axes of the slice: x: 4, y: 4, z: 4, core: 2. Of those that a mesh axis runs over, the one named last changes fastest.
Arguments:
- projector: bfloat16 [8192, 4096], P('pair', 'chol'), may hold values from -6 to 6
- chol_vectors: bfloat16 [8192, 12288], P('pair', 'chol'), may hold values from -0.078125 to 0.078125
- screen_mask: int32 [64, 96], P('pair', 'chol'), may hold values 0 or 1
- amplitudes: bfloat16 [4096, 4096], P('chol', 'pair'), may hold values from -1 to 1, as said below
- pair_energy: float32 [8192], P('pair'), may hold values from 0.5 to 4
- rank_energy: float32 [4096], P('chol'), may hold values from 0.5 to 4
Outputs:
- update: float32 [8192, 4096], P('pair', 'chol')
The draws below stay inside these ranges and needn't reach their ends.
Inputs may be any that keep to these rules, and one draw needn't show every extreme that they name: amplitudes is symmetric.
All inputs are finite; a program needn't handle non-finite values. No bound on the sum of `screen_mask` on one device may be relied on, other than what follows from the above.
Results may differ from the reference program's by a relative error of at most 0.018.
Values may be sent and summed in bfloat16 or wider, within the bound.
A program may use at most 64 MiB of HBM per device.

```python
import math
import jax
import jax.numpy as jnp
from jax import lax

RANK = 4096
NCHOL = 12288
BLOCK = 128
ROWS = 8192
N_PAIR = 8
N_CHOL = 16


def draw_amplitudes(key, part):
    key = jax.random.fold_in(key, 5)
    values = jax.random.normal(key, (RANK, RANK), jnp.float32)
    return ((values + values.T) * (0.70710678 / RANK ** 0.5)).astype(jnp.bfloat16)


def with_ends(array, own_key, low, high):
    longest = array.shape.index(max(array.shape))
    spots = []
    for shift in (0, 1):
        where = [jax.random.randint(jax.random.fold_in(own_key, axis), (), 0, length) for axis, length in enumerate(array.shape)]
        where[longest] = (where[longest] + shift) % array.shape[longest]
        spots.append(tuple(where))
    return array.at[spots[0]].set(low).at[spots[1]].set(high)


def block_levels(own_key, shape, split, low, largest):
    def one(axis_at, shards_of):
        draws = jax.random.uniform(jax.random.fold_in(jax.random.fold_in(own_key, 6), axis_at), (shards_of,), jnp.float32, low / len(split), largest / len(split))
        return jnp.repeat(jnp.exp(draws), shape[axis_at] // shards_of).reshape((-1,) + (1,) * (len(shape) - axis_at - 1))

    loudness = one(*split[0])
    for cut in split[1:]:
        loudness = loudness * one(*cut)
    return loudness


def scatter_about(rng, extent, width, most, cuts=(), kind=jnp.bfloat16):
    array = jax.random.normal(rng, extent, jnp.float32) * width
    if len(cuts) > 0:
        array = block_levels(rng, extent, cuts, -0.22, 0.18) * array
    return jnp.clip(array, min=-most, max=most).astype(kind)


def setup_inputs(seed: int = 0) -> dict:
    key_of = jax.random.split(jax.random.key(seed), 7)
    return {
        "projector": scatter_about(key_of[0], (ROWS, RANK), 1.0, 6.0, ((0, 8), (1, 16))),
        "chol_vectors": scatter_about(key_of[1], (ROWS, NCHOL), ((ROWS + NCHOL) // 4) ** -0.5, 0.078125, ((0, 8), (1, 16))),
        "screen_mask": with_ends((jax.random.randint(key_of[2], (ROWS // BLOCK, NCHOL // BLOCK), 0, 2) < 1).astype(jnp.int32), jax.random.fold_in(key_of[2], 1), 0, 1),
        "amplitudes": draw_amplitudes(jax.random.fold_in(key_of[6], 71), 0),
        "pair_energy": jnp.clip(jnp.exp(math.log(4.0) - 2.0794415 * jax.random.uniform(key_of[4], (ROWS,), jnp.float32) ** block_levels(key_of[4], (ROWS,), ((0, 8),), -0.2, 0.2)), 0.5, 4.0),
        "rank_energy": jnp.clip(jnp.exp(math.log(4.0) - 2.0794415 * jax.random.uniform(key_of[5], (RANK,), jnp.float32) ** block_levels(key_of[5], (RANK,), ((0, 16),), -0.2, 0.2)), 0.5, 4.0),
    }


def expand_mask(screen_mask):
    row_blocks, col_blocks = screen_mask.shape
    wide = jnp.broadcast_to(screen_mask[:, None, :, None], (row_blocks, BLOCK, col_blocks, BLOCK))
    return wide.reshape(row_blocks * BLOCK, col_blocks * BLOCK).astype(jnp.bfloat16)


def reference(projector, chol_vectors, screen_mask, amplitudes, pair_energy, rank_energy):
    screened = chol_vectors * expand_mask(screen_mask)
    row_dev = ROWS // N_PAIR
    proj_groups = projector.reshape(N_PAIR, row_dev, RANK)
    chol_groups = screened.reshape(N_PAIR, row_dev, NCHOL)

    def add_coupling(running, pieces):
        proj_piece, chol_piece = pieces
        partial_sum = lax.dot_general(proj_piece, chol_piece, (((0,), (0,)), ((), ())), preferred_element_type=jnp.float32)
        return running + partial_sum.astype(jnp.bfloat16).astype(jnp.float32), None

    coupling, _ = lax.scan(add_coupling, jnp.zeros((RANK, NCHOL), jnp.float32), (proj_groups, chol_groups))
    coupling = coupling.astype(jnp.bfloat16)
    image = jnp.dot(amplitudes, coupling, preferred_element_type=jnp.float32).astype(jnp.bfloat16)
    chol_dev = NCHOL // N_CHOL
    image_groups = image.reshape(RANK, N_CHOL, chol_dev).transpose(1, 0, 2)
    screen_groups = screened.reshape(ROWS, N_CHOL, chol_dev).transpose(1, 0, 2)

    def add_back(running, pieces):
        screen_piece, image_piece = pieces
        partial_sum = lax.dot_general(screen_piece, image_piece, (((1,), (1,)), ((), ())), preferred_element_type=jnp.float32)
        return running + partial_sum.astype(jnp.bfloat16).astype(jnp.float32), None

    back, _ = lax.scan(add_back, jnp.zeros((ROWS, RANK), jnp.float32), (screen_groups, image_groups))
    return (back + projector.astype(jnp.float32)) / (pair_energy[:, None] + rank_energy[None, :])
```

```python
import jax
import jax.numpy as jnp
from jax import lax
from jax.experimental import pallas as pl
from jax.experimental.pallas import tpu as pltpu
from jax.sharding import PartitionSpec as P

MESH = pl.DeviceIdType.MESH
F32, BF16 = jnp.float32, jnp.bfloat16
TASKS = ((0, 0), (0, 1), (0, 2), (1, 0), (0, 3), (1, 1), (1, 2), (1, 3))
N_SEM = 176


def kernel(mask, p_own, s_own, a_own, out, pb, ab, xp, xr, xt, sg, tp, r1, r2, tt, bt, bp, br, fin, ss, rs):
    pair, chol = lax.axis_index("pair"), lax.axis_index("chol")
    y, k, z, x = pair // 2, pair % 2, chol // 4, chol % 4

    def at(dy=0, dz=0, dx=0, core=None, yy=None, zz=None):
        ya = (y + dy + 4) % 4 if yy is None else yy
        za = (z + dz + 4) % 4 if zz is None else zz
        ka = k if core is None else core
        return {"pair": ya * 2 + ka, "chol": za * 4 + (x + dx + 4) % 4}

    sib = at(core=1 - k)
    yl, yr, zl, zr, xl, xr_ = at(dy=-1), at(dy=1), at(dz=-1), at(dz=1), at(dx=-1), at(dx=1)
    started = []
    count = [0]

    def make(src, dst, to):
        i = count[0]
        count[0] += 1
        return pltpu.make_async_remote_copy(
            src_ref=src, dst_ref=dst, send_sem=ss.at[i], recv_sem=rs.at[i], device_id=to, device_id_type=MESH
        )

    def send(src, dst, to):
        copy = make(src, dst, to)
        copy.start()
        started.append(copy)
        return copy

    barrier = pltpu.get_barrier_semaphore()
    friends = [sib, yl, yr, zl, zr, xl, xr_, at(dx=2), at(dy=2), at(dz=2), at(yy=z, zz=y, core=1 - k)]
    for friend in friends:
        pl.semaphore_signal(barrier, inc=1, device_id=friend, device_id_type=MESH)
    off = y != z

    @pl.when(off)
    def _():
        pl.semaphore_signal(barrier, inc=1, device_id=at(yy=z, zz=y), device_id_type=MESH)

    krow = pl.multiple_of(k * 1024, 1024)
    for i in range(8):
        rows = pl.ds(pl.multiple_of(krow + i * 128, 128), 128)
        for j in range(6):
            keep = mask[i, j].astype(F32)
            block = s_own[i * 128 : (i + 1) * 128, j * 128 : (j + 1) * 128].astype(F32) * keep
            sg[0, rows, j * 128 : (j + 1) * 128] = block.astype(BF16)
    zcol = pl.ds(pl.multiple_of(z * 256, 256), 256)
    krows = pl.ds(krow, 1024)
    half = [pl.ds(pl.multiple_of(krow + u * 512, 512), 512) for u in range(2)]
    pb[krows, zcol] = p_own[...]

    @pl.when(off)
    def _():
        pl.semaphore_wait(barrier, 12)

    @pl.when(y == z)
    def _():
        pl.semaphore_wait(barrier, 11)

    p_r0 = send(p_own.at[:512], pb.at[half[0], zcol], zr)
    p_l1 = send(p_own.at[512:], pb.at[half[1], zcol], zl)
    krows_a = pl.ds(pl.multiple_of(k * 128, 128), 128)
    a_dst = ab.at[:, krows_a, zcol]
    a_other = send(a_own.at[1 - k], a_dst, at(yy=z, zz=y, core=1 - k))
    a_same = make(a_own.at[k], a_dst, at(yy=z, zz=y))

    @pl.when(off)
    def _():
        a_same.start()

    @pl.when(y == z)
    def _():
        ab[:, krows_a, zcol] = a_own[k]

    p_r1 = send(p_own.at[512:], pb.at[half[1], zcol], zr)
    p_l0 = send(p_own.at[:512], pb.at[half[0], zcol], zl)
    p_sib = send(p_own, pb.at[krows, zcol], sib)
    lo, hi = slice(0, 384), slice(384, 768)
    own_lo, own_hi = sg.at[0, krows, lo], sg.at[0, krows, hi]
    s_r0 = send(own_lo, sg.at[1, krows, hi], xr_)
    s_l0 = send(own_lo, sg.at[1, krows, lo], xl)
    s_sib = send(sg.at[0, krows], sg.at[0, krows], sib)

    a_other.wait_recv()

    @pl.when(off)
    def _():
        a_same.wait_recv()

    ycol = pl.ds(pl.multiple_of(y * 256, 256), 256)
    a_all = [send(ab.at[:, :, ycol], ab.at[:, :, ycol], at(dy=d)) for d in (1, 3, 2)]

    def col(d):
        return pl.ds(pl.multiple_of((z + d + 4) % 4 * 256, 256), 256)

    def share(ref):
        return send(ref, ref, sib)

    shares = [p_sib]
    p_r0.wait_recv()
    ref = pb.at[half[0], col(-1)]
    p_fr = send(ref, ref, zr)
    shares.append(share(ref))
    p_l1.wait_recv()
    ref = pb.at[half[1], col(1)]
    p_fl = send(ref, ref, zl)
    shares.append(share(ref))
    p_r1.wait_recv()
    shares.append(share(pb.at[half[1], col(-1)]))
    p_l0.wait_recv()
    shares.append(share(pb.at[half[0], col(1)]))
    p_fr.wait_recv()
    shares.append(share(pb.at[half[0], col(2)]))
    p_fl.wait_recv()
    shares.append(share(pb.at[half[1], col(2)]))
    for copy in a_all + shares:
        copy.wait_recv()

    x_parts = []
    for h in range(2):
        part = lax.dot_general(ab[h], pb[...], (((1,), (1,)), ((), ())), preferred_element_type=F32)
        xp[h] = part.astype(BF16).reshape(4, 64, 2048)
        x_parts.append([send(xp.at[h, (x + d) % 4], xr.at[h, d - 1], at(dx=d)) for d in (1, 3, 2)])
    s_r1 = send(own_hi, sg.at[2, krows, hi], xr_)
    s_l1 = send(own_hi, sg.at[2, krows, lo], xl)
    zrow = pl.ds(pl.multiple_of(z * 64, 64), 64)
    x_all = []
    for h in range(2):
        for copy in x_parts[h]:
            copy.wait_recv()
        total = xp[h, x].astype(F32)
        for d in range(3):
            total += xr[h, d].astype(F32)
        xt[h, zrow, :] = total.astype(BF16)
        x_all.append([send(xt.at[h, zrow], xt.at[h, zrow], at(dz=d)) for d in (1, 3, 2)])

    s_sib.wait_recv()
    s_r0.wait_recv()
    s_fr = send(sg.at[1, krows, hi], sg.at[3, krows, lo], xr_)
    g1 = [share(sg.at[1, krows, hi])]
    s_l0.wait_recv()
    g1.append(share(sg.at[1, krows, lo]))

    def ready(g):
        if g == 1:
            for copy in g1:
                copy.wait_recv()
        if g == 2:
            s_r1.wait_recv()
            shared = [share(sg.at[2, krows, hi])]
            s_l1.wait_recv()
            s_fl[0] = send(sg.at[2, krows, lo], sg.at[3, krows, hi], xl)
            shared.append(share(sg.at[2, krows, lo]))
            for copy in shared:
                copy.wait_recv()
        if g == 3:
            s_fr.wait_recv()
            shared = [share(sg.at[3, krows, lo])]
            s_fl[0].wait_recv()
            shared.append(share(sg.at[3, krows, hi]))
            for copy in shared:
                copy.wait_recv()

    s_fl = [None]
    up, down, opp = (y + 1) % 4, (y + 3) % 4, (y + 2) % 4
    first, second = slice(0, 32), slice(32, 64)
    state = [{} for _ in TASKS]
    have_x, have_s = set(), {0}

    def stage0(t):
        h, g = TASKS[t]
        if h not in have_x:
            have_x.add(h)
            for copy in x_all[h]:
                copy.wait_recv()
        if g not in have_s:
            have_s.add(g)
            ready(g)
        part = jnp.dot(xt[h], sg[g], preferred_element_type=F32)
        tp[t] = part.astype(BF16).reshape(4, 64, 768)
        s = state[t]
        s["a"] = send(tp.at[t, opp, first], r1.at[t, 0], yr)
        s["b"] = send(tp.at[t, opp, second], r1.at[t, 1], yl)
        s["c"] = send(tp.at[t, up, second], r2.at[t, 0, second], yr)
        s["d"] = send(tp.at[t, down, first], r2.at[t, 1, first], yl)

    def stage1(t):
        s = state[t]
        s["a"].wait_recv()
        tp[t, up, first, :] = (tp[t, up, first, :].astype(F32) + r1[t, 0].astype(F32)).astype(BF16)
        s["e"] = send(tp.at[t, up, first], r2.at[t, 0, first], yr)
        s["b"].wait_recv()
        tp[t, down, second, :] = (tp[t, down, second, :].astype(F32) + r1[t, 1].astype(F32)).astype(BF16)
        s["f"] = send(tp.at[t, down, second], r2.at[t, 1, second], yl)

    def rows_of(index, start=0, size=64):
        return pl.ds(pl.multiple_of(index * 64 + start, 32), size)

    def stage2(t):
        h, g = TASKS[t]
        s = state[t]
        for name in "cdef":
            s[name].wait_recv()
        total = tp[t, y].astype(F32) + r2[t, 0].astype(F32) + r2[t, 1].astype(F32)
        mine = tt.at[h, g, rows_of(y)]
        tt[h, g, rows_of(y), :] = total.astype(BF16)
        s["g"] = send(mine, mine, yr)
        s["h"] = send(mine, mine, yl)

    def stage3(t):
        h, g = TASKS[t]
        s = state[t]
        s["g"].wait_recv()
        ref = tt.at[h, g, rows_of(down, 0, 32)]
        s["i"] = send(ref, ref, yr)
        s["h"].wait_recv()
        ref = tt.at[h, g, rows_of(up, 32, 32)]
        s["j"] = send(ref, ref, yl)

    done = [0, 0]
    b_parts = [None, None]

    def stage4(t):
        h, g = TASKS[t]
        s = state[t]
        s["i"].wait_recv()
        s["j"].wait_recv()
        part = lax.dot_general(tt[h, g], sg[g], (((1,), (1,)), ((), ())), preferred_element_type=F32)
        if done[h]:
            part += bt[h]
        done[h] += 1
        bt[h] = part
        if done[h] == 4:
            bp[h] = part.astype(BF16).reshape(4, 64, 2048)
            b_parts[h] = [send(bp.at[h, (z + d) % 4], br.at[h, d - 1], at(dz=d)) for d in (2, 1, 3)]

    stages = (stage0, stage1, stage2, stage3, stage4)
    for tick in range(len(TASKS) + 4):
        for back in (4, 3, 2, 1, 0):
            if 0 <= tick - back < len(TASKS):
                stages[back](tick - back)

    other = pl.ds(pl.multiple_of((1 - k) * 1024, 1024), 1024)
    finals = []
    for h in range(2):
        for copy in b_parts[h]:
            copy.wait_recv()
        total = bt[h, zrow, :]
        for d in range(3):
            total += br[h, d].astype(F32)
        bt[h, zrow, :] = total
        finals.append(send(bt.at[h, zrow, other], fin.at[h], sib))
        out[pl.ds(pl.multiple_of(k * 128 + h * 64, 64), 64), :] = bt[h, zrow, krows]
    for h in range(2):
        finals[h].wait_recv()
        out[pl.ds(pl.multiple_of((1 - k) * 128 + h * 64, 64), 64), :] = fin[h]
    for copy in started:
        copy.wait_send()

    @pl.when(off)
    def _():
        a_same.wait_send()


def local(projector, chol_vectors, screen_mask, amplitudes, pair_energy, rank_energy):
    a_own = amplitudes.T.reshape(2, 2, 2, 64, 256).transpose(1, 2, 0, 3, 4).reshape(2, 2, 128, 256)
    vmem = pl.BlockSpec(memory_space=pltpu.VMEM)
    back = pl.pallas_call(
        kernel,
        out_shape=jax.ShapeDtypeStruct((256, 1024), F32),
        in_specs=[pl.BlockSpec(memory_space=pltpu.SMEM), vmem, vmem, vmem],
        out_specs=vmem,
        scratch_shapes=[
            pltpu.VMEM((2048, 1024), BF16),
            pltpu.VMEM((2, 256, 1024), BF16),
            pltpu.VMEM((2, 4, 64, 2048), BF16),
            pltpu.VMEM((2, 3, 64, 2048), BF16),
            pltpu.VMEM((2, 256, 2048), BF16),
            pltpu.VMEM((4, 2048, 768), BF16),
            pltpu.VMEM((8, 4, 64, 768), BF16),
            pltpu.VMEM((8, 2, 32, 768), BF16),
            pltpu.VMEM((8, 2, 64, 768), BF16),
            pltpu.VMEM((2, 4, 256, 768), BF16),
            pltpu.VMEM((2, 256, 2048), F32),
            pltpu.VMEM((2, 4, 64, 2048), BF16),
            pltpu.VMEM((2, 3, 64, 2048), BF16),
            pltpu.VMEM((2, 64, 1024), F32),
            pltpu.SemaphoreType.DMA((N_SEM,)),
            pltpu.SemaphoreType.DMA((N_SEM,)),
        ],
        compiler_params=pltpu.CompilerParams(
            collective_id=0, has_side_effects=True, vmem_limit_bytes=58 * 1024 * 1024
        ),
        cost_estimate=pl.CostEstimate(flops=16 * 10**9, bytes_accessed=8 * 10**6, transcendentals=0),
    )(screen_mask, projector, chol_vectors, a_own)
    return (back.T + projector.astype(F32)) / (pair_energy[:, None] + rank_energy[None, :])


def solution(mesh):
    placed = (
        P("pair", "chol"),
        P("pair", "chol"),
        P("pair", "chol"),
        P("chol", "pair"),
        P("pair"),
        P("chol"),
    )
    return jax.shard_map(local, mesh=mesh, in_specs=placed, out_specs=P("pair", "chol"), check_vma=False)
```

```python
import jax
import jax.numpy as jnp
from jax import lax
from jax.experimental import pallas as pl
from jax.experimental.pallas import tpu as pltpu
from jax.sharding import PartitionSpec as P

MESH = pl.DeviceIdType.MESH
F32, BF16 = jnp.float32, jnp.bfloat16
TASKS = ((0, 0), (0, 1), (1, 0), (1, 1), (0, 2), (1, 2), (0, 3), (1, 3))
N_SEM = 200


def kernel(mask, p_own, s_own, a_own, out, pb, ab, xp, xr, xt, sg, tp, r1, r2, tt, bt, bp, br, fin, ss, rs):
    pair, chol = lax.axis_index("pair"), lax.axis_index("chol")
    y, k, z, x = pair // 2, pair % 2, chol // 4, chol % 4

    def at(dy=0, dz=0, dx=0, core=None, yy=None, zz=None):
        ya = (y + dy + 4) % 4 if yy is None else yy
        za = (z + dz + 4) % 4 if zz is None else zz
        ka = k if core is None else core
        return {"pair": ya * 2 + ka, "chol": za * 4 + (x + dx + 4) % 4}

    sib = at(core=1 - k)
    yl, yr, zl, zr, xl, xr_ = at(dy=-1), at(dy=1), at(dz=-1), at(dz=1), at(dx=-1), at(dx=1)
    started = []
    count = [0]

    def make(src, dst, to):
        i = count[0]
        count[0] += 1
        return pltpu.make_async_remote_copy(
            src_ref=src, dst_ref=dst, send_sem=ss.at[i], recv_sem=rs.at[i], device_id=to, device_id_type=MESH
        )

    def send(src, dst, to):
        copy = make(src, dst, to)
        copy.start()
        started.append(copy)
        return copy

    barrier = pltpu.get_barrier_semaphore()
    friends = [sib, yl, yr, zl, zr, xl, xr_, at(dx=2), at(dy=2), at(dz=2)] + [at(dx=d, core=1 - k) for d in (1, 2, 3)]
    for friend in friends:
        pl.semaphore_signal(barrier, inc=1, device_id=friend, device_id_type=MESH)
    for i in range(8):
        u, rows = i // 4, slice(i % 4 * 128, i % 4 * 128 + 128)
        for j in range(6):
            keep = mask[i, j].astype(F32)
            block = s_own[i * 128 : (i + 1) * 128, j * 128 : (j + 1) * 128].astype(F32) * keep
            sg[0, u, k, rows, j * 128 : (j + 1) * 128] = block.astype(BF16)
    zcol = pl.ds(pl.multiple_of(z * 256, 256), 256)
    for u in range(2):
        pb[u, k, :, zcol] = p_own[u * 512 : (u + 1) * 512]
    pl.semaphore_wait(barrier, len(friends))

    ycol = pl.ds(pl.multiple_of(y * 256, 256), 256)
    a_rows = pl.ds(pl.multiple_of(x * 64, 64), 64)
    a_first = count[0]
    count[0] += 4
    a_sends = []
    for j in range(2):
        for core in range(2):
            copy = pltpu.make_async_remote_copy(
                src_ref=a_own.at[core, :, :, j * 256 : (j + 1) * 256],
                dst_ref=ab.at[:, a_rows, ycol],
                send_sem=ss.at[a_first + j * 2 + core],
                recv_sem=rs.at[a_first + x],
                device_id={"pair": y * 2 + core, "chol": z * 4 + 2 * k + j},
                device_id_type=MESH,
            )
            away = jnp.logical_or(2 * k + j != x, k != core)
            a_sends.append((away, copy))

            @pl.when(away)
            def _():
                copy.start()

            @pl.when(jnp.logical_not(away))
            def _():
                ab[:, a_rows, ycol] = a_own[core, :, :, j * 256 : (j + 1) * 256]

    a256, b256 = slice(0, 256), slice(256, 512)
    p_r0 = send(pb.at[0, k, :, zcol], pb.at[0, k, :, zcol], zr)
    p_l0 = send(pb.at[0, k, :, zcol], pb.at[0, k, :, zcol], zl)
    p_ra = send(pb.at[1, k, a256, zcol], pb.at[1, k, a256, zcol], zr)
    p_lb = send(pb.at[1, k, b256, zcol], pb.at[1, k, b256, zcol], zl)
    p_sib = send(pb.at[:, k, :, zcol], pb.at[:, k, :, zcol], sib)
    lo, hi = slice(0, 384), slice(384, 768)
    s_r0 = [send(sg.at[0, u, k, :, lo], sg.at[1, u, k, :, hi], xr_) for u in range(2)]
    s_l0 = [send(sg.at[0, u, k, :, lo], sg.at[1, u, k, :, lo], xl) for u in range(2)]
    s_sib = send(sg.at[0, :, k], sg.at[0, :, k], sib)

    for source in range(4):

        @pl.when(jnp.logical_or(source != x, x // 2 != k))
        def _():
            pltpu.make_async_remote_copy(
                src_ref=ab.at[:, a_rows, ycol],
                dst_ref=ab.at[:, source * 64 : (source + 1) * 64, ycol],
                send_sem=ss.at[a_first],
                recv_sem=rs.at[a_first + source],
                device_id=xr_,
                device_id_type=MESH,
            ).wait_recv()

    a_all = [[send(ab.at[h, :, ycol], ab.at[h, :, ycol], at(dy=d)) for d in (1, 3, 2)] for h in range(2)]

    def col(d):
        return pl.ds(pl.multiple_of((z + d + 4) % 4 * 256, 256), 256)

    def share(ref):
        return send(ref, ref, sib)

    units = ((0, 0), (0, 1), (1, 0), (1, 1))
    x_parts = []

    def x_unit(h, u):
        part = lax.dot_general(
            ab[h], pb[u].reshape(1024, 1024), (((1,), (1,)), ((), ())), preferred_element_type=F32
        )
        xp[h, u] = part.astype(BF16).reshape(4, 64, 1024)
        x_parts.append([send(xp.at[h, u, (x + d) % 4], xr.at[h, u, d - 1], at(dx=d)) for d in (2, 1, 3)])

    p_r0.wait_recv()
    ref = pb.at[0, k, a256, col(-1)]
    p_fr0 = send(ref, ref, zr)
    p_l0.wait_recv()
    ref = pb.at[0, k, b256, col(1)]
    p_fl0 = send(ref, ref, zl)
    p_rb = send(pb.at[1, k, b256, zcol], pb.at[1, k, b256, zcol], zr)
    p_la = send(pb.at[1, k, a256, zcol], pb.at[1, k, a256, zcol], zl)
    shares = [p_sib, share(pb.at[0, k, :, col(-1)]), share(pb.at[0, k, :, col(1)])]
    p_ra.wait_recv()
    ref = pb.at[1, k, a256, col(-1)]
    p_fr1 = send(ref, ref, zr)
    shares1 = [share(ref)]
    p_fr0.wait_recv()
    shares.append(share(pb.at[0, k, a256, col(2)]))
    p_fl0.wait_recv()
    shares.append(share(pb.at[0, k, b256, col(2)]))
    p_lb.wait_recv()
    ref = pb.at[1, k, b256, col(1)]
    p_fl1 = send(ref, ref, zl)
    shares1.append(share(ref))
    for copy in a_all[0] + shares:
        copy.wait_recv()

    x_unit(0, 0)
    p_rb.wait_recv()
    shares1.append(share(pb.at[1, k, b256, col(-1)]))
    p_la.wait_recv()
    shares1.append(share(pb.at[1, k, a256, col(1)]))
    p_fr1.wait_recv()
    shares1.append(share(pb.at[1, k, a256, col(2)]))
    p_fl1.wait_recv()
    shares1.append(share(pb.at[1, k, b256, col(2)]))
    for copy in shares1:
        copy.wait_recv()
    x_unit(0, 1)
    for copy in a_all[1]:
        copy.wait_recv()
    x_unit(1, 0)
    x_unit(1, 1)
    s_r1 = [send(sg.at[0, u, k, :, hi], sg.at[2, u, k, :, hi], xr_) for u in range(2)]
    s_l1 = [send(sg.at[0, u, k, :, hi], sg.at[2, u, k, :, lo], xl) for u in range(2)]

    s_shares = [None, [], [], []]
    s_fr, s_fl = [], []
    for u in range(2):
        s_r0[u].wait_recv()
        s_fr.append(send(sg.at[1, u, k, :, hi], sg.at[3, u, k, :, lo], xr_))
        s_l0[u].wait_recv()
        s_shares[1].append(share(sg.at[1, u, k]))

    zrow = pl.ds(pl.multiple_of(z * 64, 64), 64)
    x_all = [[], []]

    def x_sum(h, u):
        for copy in x_parts[h * 2 + u]:
            copy.wait_recv()
        total = xp[h, u, x].astype(F32)
        for d in range(3):
            total += xr[h, u, d].astype(F32)
        mine = xt.at[h, zrow, u * 1024 : (u + 1) * 1024]
        xt[h, zrow, u * 1024 : (u + 1) * 1024] = total.astype(BF16)
        x_all[h].extend([send(mine, mine, at(dz=d)) for d in (2, 1, 3)])

    x_sum(0, 0)
    x_sum(0, 1)
    s_sib.wait_recv()
    x_sum(1, 0)

    def far(u):
        s_r1[u].wait_recv()
        s_l1[u].wait_recv()
        s_fl.append(send(sg.at[2, u, k, :, lo], sg.at[3, u, k, :, hi], xl))
        s_shares[2].append(share(sg.at[2, u, k]))

    def farther(u):
        s_fr[u].wait_recv()
        s_fl[u].wait_recv()
        s_shares[3].append(share(sg.at[3, u, k]))

    after = {0: (lambda: x_sum(1, 1),), 2: (lambda: far(0),), 3: (lambda: far(1),), 5: (lambda: farther(0), lambda: farther(1))}

    up, down, opp = (y + 1) % 4, (y + 3) % 4, (y + 2) % 4
    first, second = slice(0, 32), slice(32, 64)
    state = [{} for _ in TASKS]
    have_x, have_s = set(), {0}

    def stage0(t):
        h, g = TASKS[t]
        if h not in have_x:
            have_x.add(h)
            for copy in x_all[h]:
                copy.wait_recv()
        if g not in have_s:
            have_s.add(g)
            for copy in s_shares[g]:
                copy.wait_recv()
        part = jnp.dot(xt[h], sg[g].reshape(2048, 768), preferred_element_type=F32)
        tp[t] = part.astype(BF16).reshape(4, 64, 768)
        s = state[t]
        s["a"] = send(tp.at[t, opp, first], r1.at[t, 0], yr)
        s["b"] = send(tp.at[t, opp, second], r1.at[t, 1], yl)
        s["c"] = send(tp.at[t, up, second], r2.at[t, 0, second], yr)
        s["d"] = send(tp.at[t, down, first], r2.at[t, 1, first], yl)

    def stage1(t):
        s = state[t]
        s["a"].wait_recv()
        tp[t, up, first, :] = (tp[t, up, first, :].astype(F32) + r1[t, 0].astype(F32)).astype(BF16)
        s["e"] = send(tp.at[t, up, first], r2.at[t, 0, first], yr)
        s["b"].wait_recv()
        tp[t, down, second, :] = (tp[t, down, second, :].astype(F32) + r1[t, 1].astype(F32)).astype(BF16)
        s["f"] = send(tp.at[t, down, second], r2.at[t, 1, second], yl)

    def rows_of(index, start=0, size=64):
        return pl.ds(pl.multiple_of(index * 64 + start, 32), size)

    def stage2(t):
        h, g = TASKS[t]
        s = state[t]
        for name in "cdef":
            s[name].wait_recv()
        total = tp[t, y].astype(F32) + r2[t, 0].astype(F32) + r2[t, 1].astype(F32)
        mine = tt.at[h, g, rows_of(y)]
        tt[h, g, rows_of(y), :] = total.astype(BF16)
        s["g"] = send(mine, mine, yr)
        s["h"] = send(mine, mine, yl)

    def stage3(t):
        h, g = TASKS[t]
        s = state[t]
        s["g"].wait_recv()
        ref = tt.at[h, g, rows_of(down, 0, 32)]
        s["i"] = send(ref, ref, yr)
        s["h"].wait_recv()
        ref = tt.at[h, g, rows_of(up, 32, 32)]
        s["j"] = send(ref, ref, yl)

    done = [0, 0]
    b_parts = [None, None]

    def stage4(t):
        h, g = TASKS[t]
        s = state[t]
        s["i"].wait_recv()
        s["j"].wait_recv()
        part = lax.dot_general(tt[h, g], sg[g].reshape(2048, 768), (((1,), (1,)), ((), ())), preferred_element_type=F32)
        if done[h]:
            part += bt[h]
        done[h] += 1
        bt[h] = part
        if done[h] == 4:
            bp[h] = part.astype(BF16).reshape(4, 64, 2048)
            b_parts[h] = [send(bp.at[h, (z + d) % 4], br.at[h, d - 1], at(dz=d)) for d in (2, 1, 3)]

    stages = (stage0, stage1, stage2, stage3, stage4)
    for tick in range(len(TASKS) + 4):
        for back in (4, 3, 2, 1, 0):
            if 0 <= tick - back < len(TASKS):
                stages[back](tick - back)
        for step in after.get(tick, ()):
            step()


    def q_cols(u, core):
        return pl.ds(pl.multiple_of(u * 1024 + core * 512, 512), 512)

    finals = []

    def fin_rows(core, h):
        return pl.ds(pl.multiple_of(core * 128 + h * 64, 64), 64)

    for h in range(2):
        for copy in b_parts[h]:
            copy.wait_recv()
        total = bt[h, zrow, :]
        for d in range(3):
            total += br[h, d].astype(F32)
        bt[h, zrow, :] = total
        for u in range(2):
            cols = slice(u * 512, u * 512 + 512)
            finals.append(send(bt.at[h, zrow, q_cols(u, 1 - k)], fin.at[fin_rows(k, h), cols], sib))
            fin[fin_rows(k, h), cols] = bt[h, zrow, q_cols(u, k)]
    for copy in finals:
        copy.wait_recv()
    out[...] = fin[...].T
    for copy in started:
        copy.wait_send()

    for away, copy in a_sends:

        @pl.when(away)
        def _():
            copy.wait_send()


def local(projector, chol_vectors, screen_mask, amplitudes, pair_energy, rank_energy):
    a_own = amplitudes.reshape(2, 2, 64, 512)
    vmem = pl.BlockSpec(memory_space=pltpu.VMEM)
    back = pl.pallas_call(
        kernel,
        out_shape=jax.ShapeDtypeStruct((1024, 256), F32),
        in_specs=[pl.BlockSpec(memory_space=pltpu.SMEM), vmem, vmem, vmem],
        out_specs=vmem,
        scratch_shapes=[
            pltpu.VMEM((2, 2, 512, 1024), BF16),
            pltpu.VMEM((2, 256, 1024), BF16),
            pltpu.VMEM((2, 2, 4, 64, 1024), BF16),
            pltpu.VMEM((2, 2, 3, 64, 1024), BF16),
            pltpu.VMEM((2, 256, 2048), BF16),
            pltpu.VMEM((4, 2, 2, 512, 768), BF16),
            pltpu.VMEM((8, 4, 64, 768), BF16),
            pltpu.VMEM((8, 2, 32, 768), BF16),
            pltpu.VMEM((8, 2, 64, 768), BF16),
            pltpu.VMEM((2, 4, 256, 768), BF16),
            pltpu.VMEM((2, 256, 2048), F32),
            pltpu.VMEM((2, 4, 64, 2048), BF16),
            pltpu.VMEM((2, 3, 64, 2048), BF16),
            pltpu.VMEM((256, 1024), F32),
            pltpu.SemaphoreType.DMA((N_SEM,)),
            pltpu.SemaphoreType.DMA((N_SEM,)),
        ],
        compiler_params=pltpu.CompilerParams(
            collective_id=0, has_side_effects=True, vmem_limit_bytes=58 * 1024 * 1024
        ),
        cost_estimate=pl.CostEstimate(flops=16 * 10**9, bytes_accessed=8 * 10**6, transcendentals=0),
    )(screen_mask, projector, chol_vectors, a_own)
    return (back + projector.astype(F32)) / (pair_energy[:, None] + rank_energy[None, :])


def solution(mesh):
    placed = (
        P("pair", "chol"),
        P("pair", "chol"),
        P("pair", "chol"),
        P("chol", "pair"),
        P("pair"),
        P("chol"),
    )
    return jax.shard_map(local, mesh=mesh, in_specs=placed, out_specs=P("pair", "chol"), check_vma=False)
```

```python
import jax
import jax.numpy as jnp
from jax import lax
from jax.experimental import pallas as pl
from jax.experimental.pallas import tpu as pltpu
from jax.sharding import PartitionSpec as P

MESH = pl.DeviceIdType.MESH
F32, BF16 = jnp.float32, jnp.bfloat16
TASKS = ((0, 0), (0, 1), (1, 0), (1, 1), (0, 2), (1, 2), (0, 3), (1, 3))
N_SEM = 200


def kernel(mask, p_own, s_own, a_own, out, pb, ab, xp, xr, xt, sg, tp, r1, r2, tt, bt, bp, br, fin, ss, rs):
    pair, chol = lax.axis_index("pair"), lax.axis_index("chol")
    y, k, z, x = pair // 2, pair % 2, chol // 4, chol % 4

    def at(dy=0, dz=0, dx=0, core=None, yy=None, zz=None):
        ya = (y + dy + 4) % 4 if yy is None else yy
        za = (z + dz + 4) % 4 if zz is None else zz
        ka = k if core is None else core
        return {"pair": ya * 2 + ka, "chol": za * 4 + (x + dx + 4) % 4}

    sib = at(core=1 - k)
    yl, yr, zl, zr, xl, xr_ = at(dy=-1), at(dy=1), at(dz=-1), at(dz=1), at(dx=-1), at(dx=1)
    started = []
    count = [0]

    def make(src, dst, to):
        i = count[0]
        count[0] += 1
        return pltpu.make_async_remote_copy(
            src_ref=src, dst_ref=dst, send_sem=ss.at[i], recv_sem=rs.at[i], device_id=to, device_id_type=MESH
        )

    def send(src, dst, to):
        copy = make(src, dst, to)
        copy.start()
        started.append(copy)
        return copy

    barrier = pltpu.get_barrier_semaphore()
    friends = [sib, yl, yr, zl, zr, xl, xr_, at(dx=2), at(dy=2), at(dz=2)] + [at(dx=d, core=1 - k) for d in (1, 2, 3)]
    for friend in friends:
        pl.semaphore_signal(barrier, inc=1, device_id=friend, device_id_type=MESH)
    zcol = pl.ds(pl.multiple_of(z * 256, 256), 256)
    for u in range(2):
        pb[u, k, :, zcol] = p_own[u * 512 : (u + 1) * 512]
    pl.semaphore_wait(barrier, len(friends))

    ycol = pl.ds(pl.multiple_of(y * 256, 256), 256)
    a_rows = pl.ds(pl.multiple_of(x * 64, 64), 64)
    a_first = count[0]
    count[0] += 4
    a_sends = []
    for j in range(2):
        for core in range(2):
            copy = pltpu.make_async_remote_copy(
                src_ref=a_own.at[core, :, :, j * 256 : (j + 1) * 256],
                dst_ref=ab.at[:, a_rows, ycol],
                send_sem=ss.at[a_first + j * 2 + core],
                recv_sem=rs.at[a_first + x],
                device_id={"pair": y * 2 + core, "chol": z * 4 + 2 * k + j},
                device_id_type=MESH,
            )
            away = jnp.logical_or(2 * k + j != x, k != core)
            a_sends.append((away, copy))

            @pl.when(away)
            def _():
                copy.start()

            @pl.when(jnp.logical_not(away))
            def _():
                ab[:, a_rows, ycol] = a_own[core, :, :, j * 256 : (j + 1) * 256]

    a256, b256 = slice(0, 256), slice(256, 512)
    p_r0 = send(pb.at[0, k, :, zcol], pb.at[0, k, :, zcol], zr)
    p_l0 = send(pb.at[0, k, :, zcol], pb.at[0, k, :, zcol], zl)
    p_ra = send(pb.at[1, k, a256, zcol], pb.at[1, k, a256, zcol], zr)
    p_lb = send(pb.at[1, k, b256, zcol], pb.at[1, k, b256, zcol], zl)
    p_sib = send(pb.at[:, k, :, zcol], pb.at[:, k, :, zcol], sib)
    for i in range(8):
        u, rows = i // 4, slice(i % 4 * 128, i % 4 * 128 + 128)
        for j in range(6):
            keep = mask[i, j].astype(F32)
            block = s_own[i * 128 : (i + 1) * 128, j * 128 : (j + 1) * 128].astype(F32) * keep
            sg[0, u, k, rows, j * 128 : (j + 1) * 128] = block.astype(BF16)
    lo, hi = slice(0, 384), slice(384, 768)
    s_r0 = [send(sg.at[0, u, k, :, lo], sg.at[1, u, k, :, hi], xr_) for u in range(2)]
    s_l0 = [send(sg.at[0, u, k, :, lo], sg.at[1, u, k, :, lo], xl) for u in range(2)]
    s_sib = send(sg.at[0, :, k], sg.at[0, :, k], sib)

    for source in range(4):

        @pl.when(jnp.logical_or(source != x, x // 2 != k))
        def _():
            pltpu.make_async_remote_copy(
                src_ref=ab.at[:, a_rows, ycol],
                dst_ref=ab.at[:, source * 64 : (source + 1) * 64, ycol],
                send_sem=ss.at[a_first],
                recv_sem=rs.at[a_first + source],
                device_id=xr_,
                device_id_type=MESH,
            ).wait_recv()

    a_all = [[send(ab.at[h, :, ycol], ab.at[h, :, ycol], at(dy=d)) for d in (1, 3, 2)] for h in range(2)]

    def col(d):
        return pl.ds(pl.multiple_of((z + d + 4) % 4 * 256, 256), 256)

    def share(ref):
        return send(ref, ref, sib)

    units = ((0, 0), (0, 1), (1, 0), (1, 1))
    x_parts = []

    def x_unit(h, u):
        part = lax.dot_general(
            ab[h], pb[u].reshape(1024, 1024), (((1,), (1,)), ((), ())), preferred_element_type=F32
        )
        xp[h, u] = part.astype(BF16).reshape(4, 64, 1024)
        x_parts.append([send(xp.at[h, u, (x + d) % 4], xr.at[h, u, d - 1], at(dx=d)) for d in (2, 1, 3)])

    p_r0.wait_recv()
    ref = pb.at[0, k, a256, col(-1)]
    p_fr0 = send(ref, ref, zr)
    p_l0.wait_recv()
    ref = pb.at[0, k, b256, col(1)]
    p_fl0 = send(ref, ref, zl)
    p_rb = send(pb.at[1, k, b256, zcol], pb.at[1, k, b256, zcol], zr)
    p_la = send(pb.at[1, k, a256, zcol], pb.at[1, k, a256, zcol], zl)
    shares = [p_sib, share(pb.at[0, k, :, col(-1)]), share(pb.at[0, k, :, col(1)])]
    p_ra.wait_recv()
    ref = pb.at[1, k, a256, col(-1)]
    p_fr1 = send(ref, ref, zr)
    shares1 = [share(ref)]
    p_fr0.wait_recv()
    shares.append(share(pb.at[0, k, a256, col(2)]))
    p_fl0.wait_recv()
    shares.append(share(pb.at[0, k, b256, col(2)]))
    p_lb.wait_recv()
    ref = pb.at[1, k, b256, col(1)]
    p_fl1 = send(ref, ref, zl)
    shares1.append(share(ref))
    for copy in a_all[0] + shares:
        copy.wait_recv()

    x_unit(0, 0)
    p_rb.wait_recv()
    shares1.append(share(pb.at[1, k, b256, col(-1)]))
    p_la.wait_recv()
    shares1.append(share(pb.at[1, k, a256, col(1)]))
    p_fr1.wait_recv()
    shares1.append(share(pb.at[1, k, a256, col(2)]))
    p_fl1.wait_recv()
    shares1.append(share(pb.at[1, k, b256, col(2)]))
    for copy in shares1:
        copy.wait_recv()
    x_unit(0, 1)
    for copy in a_all[1]:
        copy.wait_recv()
    x_unit(1, 0)
    x_unit(1, 1)
    s_r1 = [send(sg.at[0, u, k, :, hi], sg.at[2, u, k, :, hi], xr_) for u in range(2)]
    s_l1 = [send(sg.at[0, u, k, :, hi], sg.at[2, u, k, :, lo], xl) for u in range(2)]

    s_shares = [None, [], [], []]
    s_fr, s_fl = [], []
    for u in range(2):
        s_r0[u].wait_recv()
        s_fr.append(send(sg.at[1, u, k, :, hi], sg.at[3, u, k, :, lo], xr_))
        s_l0[u].wait_recv()
        s_shares[1].append(share(sg.at[1, u, k]))

    zrow = pl.ds(pl.multiple_of(z * 64, 64), 64)
    x_all = [[], []]

    def x_sum(h, u):
        for copy in x_parts[h * 2 + u]:
            copy.wait_recv()
        total = xp[h, u, x].astype(F32)
        for d in range(3):
            total += xr[h, u, d].astype(F32)
        mine = xt.at[h, zrow, u * 1024 : (u + 1) * 1024]
        xt[h, zrow, u * 1024 : (u + 1) * 1024] = total.astype(BF16)
        x_all[h].extend([send(mine, mine, at(dz=d)) for d in (2, 1, 3)])

    x_sum(0, 0)
    x_sum(0, 1)
    s_sib.wait_recv()
    x_sum(1, 0)

    def far(u):
        s_r1[u].wait_recv()
        s_l1[u].wait_recv()
        s_fl.append(send(sg.at[2, u, k, :, lo], sg.at[3, u, k, :, hi], xl))
        s_shares[2].append(share(sg.at[2, u, k]))

    def farther(u):
        s_fr[u].wait_recv()
        s_fl[u].wait_recv()
        s_shares[3].append(share(sg.at[3, u, k]))

    after = {0: (lambda: x_sum(1, 1),), 2: (lambda: far(0),), 3: (lambda: far(1),), 5: (lambda: farther(0), lambda: farther(1))}

    up, down, opp = (y + 1) % 4, (y + 3) % 4, (y + 2) % 4
    first, second = slice(0, 32), slice(32, 64)
    state = [{} for _ in TASKS]
    have_x, have_s = set(), {0}

    def stage0(t):
        h, g = TASKS[t]
        if h not in have_x:
            have_x.add(h)
            for copy in x_all[h]:
                copy.wait_recv()
        if g not in have_s:
            have_s.add(g)
            for copy in s_shares[g]:
                copy.wait_recv()
        part = jnp.dot(xt[h], sg[g].reshape(2048, 768), preferred_element_type=F32)
        tp[t] = part.astype(BF16).reshape(4, 64, 768)
        s = state[t]
        s["a"] = send(tp.at[t, opp, first], r1.at[t, 0], yr)
        s["b"] = send(tp.at[t, opp, second], r1.at[t, 1], yl)
        s["c"] = send(tp.at[t, up, second], r2.at[t, 0, second], yr)
        s["d"] = send(tp.at[t, down, first], r2.at[t, 1, first], yl)

    def stage1(t):
        s = state[t]
        s["a"].wait_recv()
        tp[t, up, first, :] = (tp[t, up, first, :].astype(F32) + r1[t, 0].astype(F32)).astype(BF16)
        s["e"] = send(tp.at[t, up, first], r2.at[t, 0, first], yr)
        s["b"].wait_recv()
        tp[t, down, second, :] = (tp[t, down, second, :].astype(F32) + r1[t, 1].astype(F32)).astype(BF16)
        s["f"] = send(tp.at[t, down, second], r2.at[t, 1, second], yl)

    def rows_of(index, start=0, size=64):
        return pl.ds(pl.multiple_of(index * 64 + start, 32), size)

    def stage2(t):
        h, g = TASKS[t]
        s = state[t]
        for name in "cdef":
            s[name].wait_recv()
        total = tp[t, y].astype(F32) + r2[t, 0].astype(F32) + r2[t, 1].astype(F32)
        mine = tt.at[h, g, rows_of(y)]
        tt[h, g, rows_of(y), :] = total.astype(BF16)
        s["g"] = send(mine, mine, yr)
        s["h"] = send(mine, mine, yl)

    def stage3(t):
        h, g = TASKS[t]
        s = state[t]
        s["g"].wait_recv()
        ref = tt.at[h, g, rows_of(down, 0, 32)]
        s["i"] = send(ref, ref, yr)
        s["h"].wait_recv()
        ref = tt.at[h, g, rows_of(up, 32, 32)]
        s["j"] = send(ref, ref, yl)

    done = [0, 0]
    b_parts = [[None, None], [None, None]]

    def stage4(t):
        h, g = TASKS[t]
        s = state[t]
        s["i"].wait_recv()
        s["j"].wait_recv()
        done[h] += 1
        for u in range(2):
            cols = slice(u * 1024, u * 1024 + 1024)
            part = lax.dot_general(
                tt[h, g], sg[g, u].reshape(1024, 768), (((1,), (1,)), ((), ())), preferred_element_type=F32
            )
            if done[h] > 1:
                part += bt[h, :, cols]
            bt[h, :, cols] = part
            if done[h] == 4:
                bp[h, u] = part.astype(BF16).reshape(4, 64, 1024)
                b_parts[h][u] = [send(bp.at[h, u, (z + d) % 4], br.at[h, u, d - 1], at(dz=d)) for d in (2, 1, 3)]

    stages = (stage0, stage1, stage2, stage3, stage4)
    for tick in range(len(TASKS) + 4):
        for back in (4, 3, 2, 1, 0):
            if 0 <= tick - back < len(TASKS):
                stages[back](tick - back)
        for step in after.get(tick, ()):
            step()


    def q_cols(u, core):
        return pl.ds(pl.multiple_of(u * 1024 + core * 512, 512), 512)

    finals = []

    def fin_rows(core, h):
        return pl.ds(pl.multiple_of(core * 128 + h * 64, 64), 64)

    for h in range(2):
        for u in range(2):
            cols = slice(u * 1024, u * 1024 + 1024)
            for copy in b_parts[h][u]:
                copy.wait_recv()
            total = bt[h, zrow, cols]
            for d in range(3):
                total += br[h, u, d].astype(F32)
            bt[h, zrow, cols] = total
            cols = slice(u * 512, u * 512 + 512)
            finals.append(send(bt.at[h, zrow, q_cols(u, 1 - k)], fin.at[fin_rows(k, h), cols], sib))
            fin[fin_rows(k, h), cols] = bt[h, zrow, q_cols(u, k)]
    for copy in finals:
        copy.wait_recv()
    out[...] = fin[...].T
    for copy in started:
        copy.wait_send()

    for away, copy in a_sends:

        @pl.when(away)
        def _():
            copy.wait_send()


def local(projector, chol_vectors, screen_mask, amplitudes, pair_energy, rank_energy):
    a_own = amplitudes.reshape(2, 2, 64, 512)
    vmem = pl.BlockSpec(memory_space=pltpu.VMEM)
    back = pl.pallas_call(
        kernel,
        out_shape=jax.ShapeDtypeStruct((1024, 256), F32),
        in_specs=[pl.BlockSpec(memory_space=pltpu.SMEM), vmem, vmem, vmem],
        out_specs=vmem,
        scratch_shapes=[
            pltpu.VMEM((2, 2, 512, 1024), BF16),
            pltpu.VMEM((2, 256, 1024), BF16),
            pltpu.VMEM((2, 2, 4, 64, 1024), BF16),
            pltpu.VMEM((2, 2, 3, 64, 1024), BF16),
            pltpu.VMEM((2, 256, 2048), BF16),
            pltpu.VMEM((4, 2, 2, 512, 768), BF16),
            pltpu.VMEM((8, 4, 64, 768), BF16),
            pltpu.VMEM((8, 2, 32, 768), BF16),
            pltpu.VMEM((8, 2, 64, 768), BF16),
            pltpu.VMEM((2, 4, 256, 768), BF16),
            pltpu.VMEM((2, 256, 2048), F32),
            pltpu.VMEM((2, 2, 4, 64, 1024), BF16),
            pltpu.VMEM((2, 2, 3, 64, 1024), BF16),
            pltpu.VMEM((256, 1024), F32),
            pltpu.SemaphoreType.DMA((N_SEM,)),
            pltpu.SemaphoreType.DMA((N_SEM,)),
        ],
        compiler_params=pltpu.CompilerParams(
            collective_id=0, has_side_effects=True, vmem_limit_bytes=58 * 1024 * 1024
        ),
        cost_estimate=pl.CostEstimate(flops=16 * 10**9, bytes_accessed=8 * 10**6, transcendentals=0),
    )(screen_mask, projector, chol_vectors, a_own)
    return (back + projector.astype(F32)) / (pair_energy[:, None] + rank_energy[None, :])


def solution(mesh):
    placed = (
        P("pair", "chol"),
        P("pair", "chol"),
        P("pair", "chol"),
        P("chol", "pair"),
        P("pair"),
        P("chol"),
    )
    return jax.shard_map(local, mesh=mesh, in_specs=placed, out_specs=P("pair", "chol"), check_vma=False)
```

```python
import jax
import jax.numpy as jnp
from jax import lax
from jax.experimental import pallas as pl
from jax.experimental.pallas import tpu as pltpu
from jax.sharding import PartitionSpec as P

MESH = pl.DeviceIdType.MESH
F32, BF16 = jnp.float32, jnp.bfloat16
TASKS = ((0, 0), (0, 1), (1, 0), (1, 1), (0, 2), (1, 2), (0, 3), (1, 3))
N_SEM = 200


def kernel(mask, p_own, s_own, a_own, out, pb, ab, xp, xr, xt, sg, tp, r1, r2, tt, bt, bp, br, fin, ss, rs):
    pair, chol = lax.axis_index("pair"), lax.axis_index("chol")
    y, k, z, x = pair // 2, pair % 2, chol // 4, chol % 4

    def at(dy=0, dz=0, dx=0, core=None, yy=None, zz=None):
        ya = (y + dy + 4) % 4 if yy is None else yy
        za = (z + dz + 4) % 4 if zz is None else zz
        ka = k if core is None else core
        return {"pair": ya * 2 + ka, "chol": za * 4 + (x + dx + 4) % 4}

    sib = at(core=1 - k)
    yl, yr, zl, zr, xl, xr_ = at(dy=-1), at(dy=1), at(dz=-1), at(dz=1), at(dx=-1), at(dx=1)
    started = []
    count = [0]

    def make(src, dst, to):
        i = count[0]
        count[0] += 1
        return pltpu.make_async_remote_copy(
            src_ref=src, dst_ref=dst, send_sem=ss.at[i], recv_sem=rs.at[i], device_id=to, device_id_type=MESH
        )

    def send(src, dst, to):
        copy = make(src, dst, to)
        copy.start()
        started.append(copy)
        return copy

    barrier = pltpu.get_barrier_semaphore()
    friends = [sib, yl, yr, zl, zr, xl, xr_, at(dx=2), at(dy=2), at(dz=2)] + [at(dx=d, core=1 - k) for d in (1, 2, 3)]
    for friend in friends:
        pl.semaphore_signal(barrier, inc=1, device_id=friend, device_id_type=MESH)
    zcol = pl.ds(pl.multiple_of(z * 256, 256), 256)
    for u in range(2):
        pb[u, k, :, zcol] = p_own[u * 512 : (u + 1) * 512]
    pl.semaphore_wait(barrier, len(friends))

    ycol = pl.ds(pl.multiple_of(y * 256, 256), 256)
    a_rows = pl.ds(pl.multiple_of(x * 64, 64), 64)
    a_first = count[0]
    count[0] += 4
    a_sends = []
    for j in range(2):
        for core in range(2):
            copy = pltpu.make_async_remote_copy(
                src_ref=a_own.at[core, :, :, j * 256 : (j + 1) * 256],
                dst_ref=ab.at[:, a_rows, ycol],
                send_sem=ss.at[a_first + j * 2 + core],
                recv_sem=rs.at[a_first + x],
                device_id={"pair": y * 2 + core, "chol": z * 4 + 2 * k + j},
                device_id_type=MESH,
            )
            away = jnp.logical_or(2 * k + j != x, k != core)
            a_sends.append((away, copy))

            @pl.when(away)
            def _():
                copy.start()

            @pl.when(jnp.logical_not(away))
            def _():
                ab[:, a_rows, ycol] = a_own[core, :, :, j * 256 : (j + 1) * 256]

    a256, b256 = slice(0, 256), slice(256, 512)
    p_r0 = send(pb.at[0, k, :, zcol], pb.at[0, k, :, zcol], zr)
    p_l0 = send(pb.at[0, k, :, zcol], pb.at[0, k, :, zcol], zl)
    p_ra = send(pb.at[1, k, a256, zcol], pb.at[1, k, a256, zcol], zr)
    p_lb = send(pb.at[1, k, b256, zcol], pb.at[1, k, b256, zcol], zl)
    p_sib = send(pb.at[:, k, :, zcol], pb.at[:, k, :, zcol], sib)
    for i in range(8):
        u, rows = i // 4, slice(i % 4 * 128, i % 4 * 128 + 128)
        for j in range(6):
            keep = mask[i, j].astype(F32)
            block = s_own[i * 128 : (i + 1) * 128, j * 128 : (j + 1) * 128].astype(F32) * keep
            sg[0, u, k, rows, j * 128 : (j + 1) * 128] = block.astype(BF16)
    lo, hi = slice(0, 384), slice(384, 768)
    s_r0 = [send(sg.at[0, u, k, :, lo], sg.at[1, u, k, :, hi], xr_) for u in range(2)]
    s_l0 = [send(sg.at[0, u, k, :, lo], sg.at[1, u, k, :, lo], xl) for u in range(2)]
    s_sib = send(sg.at[0, :, k], sg.at[0, :, k], sib)

    for source in range(4):

        @pl.when(jnp.logical_or(source != x, x // 2 != k))
        def _():
            pltpu.make_async_remote_copy(
                src_ref=ab.at[:, a_rows, ycol],
                dst_ref=ab.at[:, source * 64 : (source + 1) * 64, ycol],
                send_sem=ss.at[a_first],
                recv_sem=rs.at[a_first + source],
                device_id=xr_,
                device_id_type=MESH,
            ).wait_recv()

    a_all = [[send(ab.at[h, :, ycol], ab.at[h, :, ycol], at(dy=d)) for d in (1, 3, 2)] for h in range(2)]

    def col(d):
        return pl.ds(pl.multiple_of((z + d + 4) % 4 * 256, 256), 256)

    def share(ref):
        return send(ref, ref, sib)

    units = ((0, 0), (0, 1), (1, 0), (1, 1))
    x_parts = []

    def x_unit(h, u):
        part = lax.dot_general(
            ab[h], pb[u].reshape(1024, 1024), (((1,), (1,)), ((), ())), preferred_element_type=F32
        )
        xp[h, u] = part.astype(BF16).reshape(4, 64, 1024)
        x_parts.append([send(xp.at[h, u, (x + d) % 4], xr.at[h, u, d - 1], at(dx=d)) for d in (2, 1, 3)])

    p_r0.wait_recv()
    ref = pb.at[0, k, a256, col(-1)]
    p_fr0 = send(ref, ref, zr)
    p_l0.wait_recv()
    ref = pb.at[0, k, b256, col(1)]
    p_fl0 = send(ref, ref, zl)
    p_rb = send(pb.at[1, k, b256, zcol], pb.at[1, k, b256, zcol], zr)
    p_la = send(pb.at[1, k, a256, zcol], pb.at[1, k, a256, zcol], zl)
    shares = [p_sib, share(pb.at[0, k, :, col(-1)]), share(pb.at[0, k, :, col(1)])]
    p_ra.wait_recv()
    ref = pb.at[1, k, a256, col(-1)]
    p_fr1 = send(ref, ref, zr)
    shares1 = [share(ref)]
    p_fr0.wait_recv()
    shares.append(share(pb.at[0, k, a256, col(2)]))
    p_fl0.wait_recv()
    shares.append(share(pb.at[0, k, b256, col(2)]))
    p_lb.wait_recv()
    ref = pb.at[1, k, b256, col(1)]
    p_fl1 = send(ref, ref, zl)
    shares1.append(share(ref))
    for copy in a_all[0] + shares:
        copy.wait_recv()

    x_unit(0, 0)
    p_rb.wait_recv()
    shares1.append(share(pb.at[1, k, b256, col(-1)]))
    p_la.wait_recv()
    shares1.append(share(pb.at[1, k, a256, col(1)]))
    p_fr1.wait_recv()
    shares1.append(share(pb.at[1, k, a256, col(2)]))
    p_fl1.wait_recv()
    shares1.append(share(pb.at[1, k, b256, col(2)]))
    for copy in shares1:
        copy.wait_recv()
    x_unit(0, 1)
    for copy in a_all[1]:
        copy.wait_recv()
    x_unit(1, 0)
    x_unit(1, 1)
    s_r1 = [send(sg.at[0, u, k, :, hi], sg.at[2, u, k, :, hi], xr_) for u in range(2)]
    s_l1 = [send(sg.at[0, u, k, :, hi], sg.at[2, u, k, :, lo], xl) for u in range(2)]

    s_shares = [None, [], [], []]
    s_fr, s_fl = [], []
    for u in range(2):
        s_r0[u].wait_recv()
        s_fr.append(send(sg.at[1, u, k, :, hi], sg.at[3, u, k, :, lo], xr_))
        s_l0[u].wait_recv()
        s_shares[1].append(share(sg.at[1, u, k]))

    zrow = pl.ds(pl.multiple_of(z * 64, 64), 64)
    x_all = [[], []]

    def x_sum(h, u):
        for copy in x_parts[h * 2 + u]:
            copy.wait_recv()
        total = xp[h, u, x].astype(F32)
        for d in range(3):
            total += xr[h, u, d].astype(F32)
        mine = xt.at[h, zrow, u * 1024 : (u + 1) * 1024]
        xt[h, zrow, u * 1024 : (u + 1) * 1024] = total.astype(BF16)
        x_all[h].extend([send(mine, mine, at(dz=d)) for d in (2, 1, 3)])

    x_sum(0, 0)
    x_sum(0, 1)
    s_sib.wait_recv()
    x_sum(1, 0)

    def far(u):
        s_r1[u].wait_recv()
        s_l1[u].wait_recv()
        s_fl.append(send(sg.at[2, u, k, :, lo], sg.at[3, u, k, :, hi], xl))
        s_shares[2].append(share(sg.at[2, u, k]))

    def farther(u):
        s_fr[u].wait_recv()
        s_fl[u].wait_recv()
        s_shares[3].append(share(sg.at[3, u, k]))

    after = {
        0: (lambda: x_sum(1, 1),),
        1: (lambda: far(0),),
        3: (lambda: far(1),),
        4: (lambda: farther(0),),
        5: (lambda: farther(1),),
    }

    up, down, opp = (y + 1) % 4, (y + 3) % 4, (y + 2) % 4
    first, second = slice(0, 32), slice(32, 64)
    state = [{} for _ in TASKS]
    have_x, have_s = set(), {0}

    def stage0(t):
        h, g = TASKS[t]
        if h not in have_x:
            have_x.add(h)
            for copy in x_all[h]:
                copy.wait_recv()
        if g not in have_s:
            have_s.add(g)
            for copy in s_shares[g]:
                copy.wait_recv()
        part = jnp.dot(xt[h], sg[g].reshape(2048, 768), preferred_element_type=F32)
        tp[t] = part.astype(BF16).reshape(4, 64, 768)
        s = state[t]
        s["a"] = send(tp.at[t, opp, first], r1.at[t, 0], yr)
        s["b"] = send(tp.at[t, opp, second], r1.at[t, 1], yl)
        s["c"] = send(tp.at[t, up, second], r2.at[t, 0, second], yr)
        s["d"] = send(tp.at[t, down, first], r2.at[t, 1, first], yl)

    def stage1(t):
        s = state[t]
        s["a"].wait_recv()
        tp[t, up, first, :] = (tp[t, up, first, :].astype(F32) + r1[t, 0].astype(F32)).astype(BF16)
        s["e"] = send(tp.at[t, up, first], r2.at[t, 0, first], yr)
        s["b"].wait_recv()
        tp[t, down, second, :] = (tp[t, down, second, :].astype(F32) + r1[t, 1].astype(F32)).astype(BF16)
        s["f"] = send(tp.at[t, down, second], r2.at[t, 1, second], yl)

    def rows_of(index, start=0, size=64):
        return pl.ds(pl.multiple_of(index * 64 + start, 32), size)

    def stage2(t):
        h, g = TASKS[t]
        s = state[t]
        for name in "cdef":
            s[name].wait_recv()
        total = tp[t, y].astype(F32) + r2[t, 0].astype(F32) + r2[t, 1].astype(F32)
        mine = tt.at[h, g, rows_of(y)]
        tt[h, g, rows_of(y), :] = total.astype(BF16)
        s["g"] = send(mine, mine, yr)
        s["h"] = send(mine, mine, yl)

    def stage3(t):
        h, g = TASKS[t]
        s = state[t]
        s["g"].wait_recv()
        ref = tt.at[h, g, rows_of(down, 0, 32)]
        s["i"] = send(ref, ref, yr)
        s["h"].wait_recv()
        ref = tt.at[h, g, rows_of(up, 32, 32)]
        s["j"] = send(ref, ref, yl)

    done = [0, 0]
    b_parts = [[None, None], [None, None]]

    def stage4(t):
        h, g = TASKS[t]
        s = state[t]
        s["i"].wait_recv()
        s["j"].wait_recv()
        done[h] += 1
        for u in range(2):
            cols = slice(u * 1024, u * 1024 + 1024)
            part = lax.dot_general(
                tt[h, g], sg[g, u].reshape(1024, 768), (((1,), (1,)), ((), ())), preferred_element_type=F32
            )
            if done[h] > 1:
                part += bt[h, :, cols]
            bt[h, :, cols] = part
            if done[h] == 4:
                bp[h, u] = part.astype(BF16).reshape(4, 64, 1024)
                b_parts[h][u] = [send(bp.at[h, u, (z + d) % 4], br.at[h, u, d - 1], at(dz=d)) for d in (2, 1, 3)]

    stages = (stage0, stage1, stage2, stage3, stage4)
    for tick in range(len(TASKS) + 4):
        for back in (4, 3, 2, 1, 0):
            if 0 <= tick - back < len(TASKS):
                stages[back](tick - back)
        for step in after.get(tick, ()):
            step()


    def q_cols(u, core):
        return pl.ds(pl.multiple_of(u * 1024 + core * 512, 512), 512)

    finals = []

    def fin_rows(core, h):
        return pl.ds(pl.multiple_of(core * 128 + h * 64, 64), 64)

    for h in range(2):
        for u in range(2):
            cols = slice(u * 1024, u * 1024 + 1024)
            for copy in b_parts[h][u]:
                copy.wait_recv()
            total = bt[h, zrow, cols]
            for d in range(3):
                total += br[h, u, d].astype(F32)
            bt[h, zrow, cols] = total
            cols = slice(u * 512, u * 512 + 512)
            finals.append(send(bt.at[h, zrow, q_cols(u, 1 - k)], fin.at[fin_rows(k, h), cols], sib))
            fin[fin_rows(k, h), cols] = bt[h, zrow, q_cols(u, k)]
    for copy in finals:
        copy.wait_recv()
    out[...] = fin[...].T
    for copy in started:
        copy.wait_send()

    for away, copy in a_sends:

        @pl.when(away)
        def _():
            copy.wait_send()


def local(projector, chol_vectors, screen_mask, amplitudes, pair_energy, rank_energy):
    a_own = amplitudes.reshape(2, 2, 64, 512)
    vmem = pl.BlockSpec(memory_space=pltpu.VMEM)
    back = pl.pallas_call(
        kernel,
        out_shape=jax.ShapeDtypeStruct((1024, 256), F32),
        in_specs=[pl.BlockSpec(memory_space=pltpu.SMEM), vmem, vmem, vmem],
        out_specs=vmem,
        scratch_shapes=[
            pltpu.VMEM((2, 2, 512, 1024), BF16),
            pltpu.VMEM((2, 256, 1024), BF16),
            pltpu.VMEM((2, 2, 4, 64, 1024), BF16),
            pltpu.VMEM((2, 2, 3, 64, 1024), BF16),
            pltpu.VMEM((2, 256, 2048), BF16),
            pltpu.VMEM((4, 2, 2, 512, 768), BF16),
            pltpu.VMEM((8, 4, 64, 768), BF16),
            pltpu.VMEM((8, 2, 32, 768), BF16),
            pltpu.VMEM((8, 2, 64, 768), BF16),
            pltpu.VMEM((2, 4, 256, 768), BF16),
            pltpu.VMEM((2, 256, 2048), F32),
            pltpu.VMEM((2, 2, 4, 64, 1024), BF16),
            pltpu.VMEM((2, 2, 3, 64, 1024), BF16),
            pltpu.VMEM((256, 1024), F32),
            pltpu.SemaphoreType.DMA((N_SEM,)),
            pltpu.SemaphoreType.DMA((N_SEM,)),
        ],
        compiler_params=pltpu.CompilerParams(
            collective_id=0, has_side_effects=True, vmem_limit_bytes=58 * 1024 * 1024
        ),
        cost_estimate=pl.CostEstimate(flops=16 * 10**9, bytes_accessed=8 * 10**6, transcendentals=0),
    )(screen_mask, projector, chol_vectors, a_own)
    return (back + projector.astype(F32)) / (pair_energy[:, None] + rank_energy[None, :])


def solution(mesh):
    placed = (
        P("pair", "chol"),
        P("pair", "chol"),
        P("pair", "chol"),
        P("chol", "pair"),
        P("pair"),
        P("chol"),
    )
    return jax.shard_map(local, mesh=mesh, in_specs=placed, out_specs=P("pair", "chol"), check_vma=False)
```
